32 devices in a mesh: groups: 2 (over y), site: 4 (over z), member: 4 (over x, core).
Axes of the slice: x: 2, y: 2, z: 4, core: 2. Of those that a mesh axis runs over, the one named last changes fastest.
Arguments:
- tokens: bfloat16 [2048, 2880], P(('groups', 'site', 'member')), parts along dimension 0, may hold values from -6 to 6
- expert_ids: int32 [2048, 4], P(('groups', 'site', 'member')), parts along dimension 0, may hold values from 0 to 15, as said below
- route_weights: bfloat16 [2048, 4], P(('groups', 'site', 'member')), parts along dimension 0, may hold values from 0.049804688 to 1
- w_gate: bfloat16 [16, 2880, 2880], P(('site', 'member')), may hold values from -0.109375 to 0.109375
- w_up: bfloat16 [16, 2880, 2880], P(('site', 'member')), may hold values from -0.109375 to 0.109375
- w_down: bfloat16 [16, 2880, 2880], P(('site', 'member')), may hold values from -0.109375 to 0.109375
Outputs:
- mixed: bfloat16 [2048, 2880], P(('groups', 'site', 'member')), parts along dimension 0
The draws below stay inside these ranges and needn't reach their ends.
There are 2 independent parts, one for each index of `groups`. The reference program is written for one: setup_inputs(seed, part) draws one part's arguments, and reference() takes and returns one part's arrays. A program takes and returns all parts, laid end to end along the dimension named above; an argument that names none is the same for every part. Nothing has to cross between parts.
Inputs may be any that keep to these rules, and one draw needn't show every extreme that they name: `expert_ids`: each row names 4 different experts. At most 18 of the 64 tokens of one device name any one expert.
All inputs are finite; a program needn't handle non-finite values.
Results may differ from the reference program's by a relative error of at most 0.014.
Values may be sent and summed in bfloat16 or wider, within the bound.
A program may use at most 192 MiB of HBM per device.

```python
import math
import jax
import jax.numpy as jnp
import numpy as np
from jax import lax

D = 2880
FF = 2880
TOP = 4
TOK_DEV = 64
EXP_SITE = 4
EXPERTS = 16
SPLIT = 1
FFS = 2880
TOKENS = 1024
MOST = 18
N_SITE = 4
N_MEMBER = 4


def draw_expert_ids(key, part):
    device_total = N_SITE * N_MEMBER
    expert_total = EXP_SITE * N_SITE
    mean_load = TOK_DEV * TOP // expert_total
    spread = MOST - mean_load
    pair_total = expert_total // 2
    rest_pairs = pair_total - EXP_SITE
    first_table = np.concatenate([np.arange(EXP_SITE), 2 * EXP_SITE + 2 * np.arange(rest_pairs)]).astype(np.int32)
    second_table = np.concatenate([EXP_SITE + np.arange(EXP_SITE), 2 * EXP_SITE + 2 * np.arange(rest_pairs) + 1]).astype(np.int32)
    pair_first = jnp.asarray(first_table, jnp.int32)
    pair_second = jnp.asarray(second_table, jnp.int32)
    hot_expert = jax.random.randint(jax.random.fold_in(key, 11), (), 0, expert_total)
    hot_member = jax.random.randint(jax.random.fold_in(key, 12), (), 0, N_MEMBER)
    hot_site = hot_expert // EXP_SITE
    site_first = hot_site * EXP_SITE + (hot_expert % EXP_SITE + jnp.arange(EXP_SITE, dtype=jnp.int32)) % EXP_SITE
    pair_ids = jnp.arange(pair_total, dtype=jnp.int32)

    def device_ids(device):
        device_key = jax.random.fold_in(jax.random.fold_in(key, 13), device)
        key_order, key_delta, key_perm, key_roll = jax.random.split(device_key, 4)
        others_rank = jax.random.permutation(key_order, expert_total - EXP_SITE).astype(jnp.int32)
        others = jnp.where(others_rank >= hot_site * EXP_SITE, others_rank + EXP_SITE, others_rank)
        expert_order = jnp.concatenate([site_first.astype(jnp.int32), others.astype(jnp.int32)])
        deltas = jax.random.randint(key_delta, (pair_total,), -spread, spread + 1)
        forced = (pair_ids == 0) | (device % N_MEMBER == hot_member) & (pair_ids < EXP_SITE)
        deltas = jnp.where(forced, spread, deltas)
        counts = jnp.zeros((expert_total,), jnp.int32).at[pair_first].set(mean_load + deltas).at[pair_second].set(mean_load - deltas)
        tickets = jnp.repeat(expert_order, counts, total_repeat_length=TOK_DEV * TOP)
        layout = tickets.reshape(TOP, TOK_DEV).T
        permuted = layout[jax.random.permutation(key_perm, TOK_DEV)]
        shifts = jax.random.randint(key_roll, (TOK_DEV, 1), 0, TOP)
        columns = (jnp.arange(TOP, dtype=jnp.int32)[None, :] + shifts) % TOP
        return jnp.take_along_axis(permuted, columns, axis=1)
    all_devices = jax.vmap(device_ids)(jnp.arange(device_total, dtype=jnp.int32))
    return all_devices.reshape(device_total * TOK_DEV, TOP).astype(jnp.int32)


def levels(own_key, extent, pieces, low, top_value):
    loudness, own = 1.0, jax.random.fold_in(own_key, 6)
    for axis_at, shards_of in pieces:
        steps = jnp.exp(jax.random.uniform(jax.random.fold_in(own, axis_at), (shards_of,), jnp.float32, low / len(pieces), top_value / len(pieces)))
        loudness = loudness * jnp.repeat(steps, extent[axis_at] // shards_of).reshape([-1 if axis == axis_at else 1 for axis in range(len(extent))])
    return loudness


def scatter_about(stream_key, dims, width, reach, shards=(), kind=jnp.bfloat16):
    values = width * jax.random.normal(stream_key, dims, jnp.float32)
    if shards:
        values = values * levels(stream_key, dims, shards, -0.22, 0.18)
    return jnp.clip(values, -reach, reach).astype(kind)


def setup_inputs(seed: int = 0, part: int = 0) -> dict:
    seeds = jax.random.split(jax.random.key(seed), 7)
    own_keys = jax.random.split(jax.random.fold_in(seeds[6], part), 7)
    tokens = scatter_about(own_keys[0], (TOKENS, D), 1.0, 6.0, ((0, 16),))
    expert_ids = draw_expert_ids(jax.random.fold_in(jax.random.fold_in(seeds[6], part), 71), part)
    route_weights = jnp.clip(jnp.exp(math.log(1.0) - 2.9996462 * jax.random.uniform(own_keys[2], (TOKENS, TOP), jnp.float32) ** levels(own_keys[2], (TOKENS, TOP), ((0, 16),), -0.2, 0.2)), 0.049804688, 1.0).astype(jnp.bfloat16)
    w_gate = scatter_about(seeds[3], (EXPERTS * SPLIT, D, FFS), D ** -0.5, 0.109375, ((0, 16),))
    w_up = scatter_about(seeds[4], (EXPERTS * SPLIT, D, FFS), D ** -0.5, 0.109375, ((0, 16),))
    w_down = scatter_about(seeds[5], (EXPERTS * SPLIT, FFS, D), FF ** -0.5, 0.109375, ((0, 16),))
    return dict(tokens=tokens, expert_ids=expert_ids, route_weights=route_weights, w_gate=w_gate, w_up=w_up, w_down=w_down)


alpha_glu = 1.702


def expert_partial(inputs, gate_weight, up_weight, down_weight):
    gate_value = jnp.dot(inputs, gate_weight, preferred_element_type=jnp.float32)
    up_value = jnp.dot(inputs, up_weight, preferred_element_type=jnp.float32)
    hidden = ((up_value + 1.0) * gate_value * jax.nn.sigmoid(alpha_glu * gate_value)).astype(jnp.bfloat16)
    return jnp.dot(hidden, down_weight, preferred_element_type=jnp.float32).astype(jnp.bfloat16)


def reference(tokens, expert_ids, route_weights, w_gate, w_up, w_down):
    count_tokens = tokens.shape[0]
    top_count = expert_ids.shape[1]
    split_count = N_MEMBER // EXP_SITE
    capacity = N_SITE * N_MEMBER * MOST
    flat_ids = expert_ids.reshape(-1)
    flat_weight = route_weights.reshape(-1).astype(jnp.float32)
    flat_token = jnp.arange(count_tokens * top_count, dtype=jnp.int32) // top_count

    def one_site(running_sum, site_number):
        site_total = jnp.zeros(tokens.shape, jnp.float32)
        for within in range(EXP_SITE):
            expert = site_number * EXP_SITE + within
            chosen = flat_ids == expert
            position = jnp.cumsum(chosen.astype(jnp.int32)) - 1
            target = jnp.where(chosen, position, capacity).astype(jnp.int32)
            row_ids = jnp.zeros((capacity,), jnp.int32).at[target].set(flat_token, mode="drop")
            row_weight = jnp.zeros((capacity,), jnp.float32).at[target].set(flat_weight, mode="drop")
            inputs = tokens[row_ids]
            summed = jnp.zeros((capacity, tokens.shape[1]), jnp.float32)
            for shard_index in range(split_count):
                weight_index = expert * split_count + shard_index
                partial_out = expert_partial(inputs, w_gate[weight_index], w_up[weight_index], w_down[weight_index])
                summed = summed + partial_out.astype(jnp.float32)
            site_total = site_total.at[row_ids].add(row_weight[:, None] * summed)
        rounded = lax.optimization_barrier(site_total.astype(jnp.bfloat16))
        return running_sum + rounded.astype(jnp.float32), site_number

    start_sum = jnp.zeros(tokens.shape, jnp.float32)
    running_sum, unused = lax.scan(one_site, start_sum, jnp.arange(N_SITE, dtype=jnp.int32))
    return running_sum.astype(jnp.bfloat16)
```

```python
import jax
import jax.numpy as jnp
from jax import lax
from jax.sharding import PartitionSpec as P

EXP_SITE = 4
ALPHA = 1.702
AXES = ("site", "member")


def routing(expert_ids, route_weights, experts, most):
    count = expert_ids.shape[0]
    columns = lax.broadcasted_iota(jnp.int32, (1, 1, experts), 2)
    matches = expert_ids[:, :, None] == columns
    hit = jnp.any(matches, axis=1)
    table = jnp.sum(jnp.where(matches, route_weights[:, :, None].astype(jnp.float32), 0.0), axis=1)
    row = lax.broadcasted_iota(jnp.int32, (count, count), 0)
    col = lax.broadcasted_iota(jnp.int32, (count, count), 1)
    before = (col < row).astype(jnp.bfloat16)
    position = lax.dot_general(
        hit.astype(jnp.bfloat16), before, (((0,), (1,)), ((), ())), preferred_element_type=jnp.float32
    ).astype(jnp.int32)
    slot = lax.broadcasted_iota(jnp.int32, (experts, most, count), 1)
    chosen = (position[:, None, :] == slot) & hit.T[:, None, :]
    select = chosen.astype(jnp.bfloat16)
    weights = jnp.where(chosen, table.T[:, None, :], 0.0).astype(jnp.bfloat16)
    return select, weights


def expert_apply(rows, gate_weight, up_weight, down_weight):
    gate = jnp.dot(rows, gate_weight, preferred_element_type=jnp.float32)
    up = jnp.dot(rows, up_weight, preferred_element_type=jnp.float32)
    hidden = ((up + 1.0) * gate * jax.nn.sigmoid(ALPHA * gate)).astype(jnp.bfloat16)
    return jnp.dot(hidden, down_weight, preferred_element_type=jnp.float32).astype(jnp.bfloat16)


def body(tokens, expert_ids, route_weights, w_gate, w_up, w_down):
    experts = EXP_SITE * lax.axis_size("site")
    split = lax.axis_size("member") // EXP_SITE
    count, width = tokens.shape
    mean_rows = count * expert_ids.shape[1] // experts
    most = mean_rows + max(1, mean_rows // 8)
    select, weights = routing(expert_ids, route_weights, experts, most)
    packed = jnp.dot(select.reshape(experts * most, count), tokens, preferred_element_type=jnp.float32)
    packed = packed.astype(jnp.bfloat16).reshape(experts, most, width)
    outgoing = jnp.repeat(packed, split, axis=0)
    received = lax.all_to_all(outgoing, AXES, split_axis=0, concat_axis=0, tiled=True)
    produced = expert_apply(received.reshape(-1, width), w_gate[0], w_up[0], w_down[0])
    returned = lax.all_to_all(produced.reshape(received.shape), AXES, split_axis=0, concat_axis=0, tiled=True)
    spread = jnp.repeat(weights, split, axis=0).reshape(experts * split * most, count)
    mixed = lax.dot_general(
        spread, returned.reshape(-1, width), (((0,), (0,)), ((), ())), preferred_element_type=jnp.float32
    )
    return mixed.astype(jnp.bfloat16)


def solution(mesh):
    rows = P(("groups", "site", "member"), None)
    held = P(("site", "member"), None, None)
    return jax.shard_map(
        body,
        mesh=mesh,
        in_specs=(rows, rows, rows, held, held, held),
        out_specs=rows,
        check_vma=False,
    )
```

```python
import jax
import jax.numpy as jnp
from jax import lax
from jax.sharding import PartitionSpec as P

EXP_SITE = 4
ALPHA = 1.702
AXES = ("site", "member")
ROWS, LANES = 16, 128


def routing(expert_ids, route_weights, experts, most):
    count = expert_ids.shape[0]
    columns = lax.broadcasted_iota(jnp.int32, (1, 1, experts), 2)
    matches = expert_ids[:, :, None] == columns
    hit = jnp.any(matches, axis=1)
    table = jnp.sum(jnp.where(matches, route_weights[:, :, None].astype(jnp.float32), 0.0), axis=1)
    row = lax.broadcasted_iota(jnp.int32, (count, count), 0)
    col = lax.broadcasted_iota(jnp.int32, (count, count), 1)
    before = (col < row).astype(jnp.bfloat16)
    position = lax.dot_general(
        hit.astype(jnp.bfloat16), before, (((0,), (1,)), ((), ())), preferred_element_type=jnp.float32
    ).astype(jnp.int32)
    slot = lax.broadcasted_iota(jnp.int32, (experts, most, count), 1)
    chosen = (position[:, None, :] == slot) & hit.T[:, None, :]
    select = chosen.astype(jnp.bfloat16)
    weights = jnp.where(chosen, table.T[:, None, :], 0.0).astype(jnp.bfloat16)
    return select, weights


def expert_apply(rows, gate_weight, up_weight, down_weight):
    gate = jnp.dot(rows, gate_weight, preferred_element_type=jnp.float32)
    up = jnp.dot(rows, up_weight, preferred_element_type=jnp.float32)
    hidden = ((up + 1.0) * gate * jax.nn.sigmoid(ALPHA * gate)).astype(jnp.bfloat16)
    return jnp.dot(hidden, down_weight, preferred_element_type=jnp.float32).astype(jnp.bfloat16)


def fold_plan(most, width):
    extra = most % ROWS
    if most > ROWS and extra and ROWS % extra == 0 and most // ROWS == 1:
        pieces = ROWS // extra
        return ROWS, pieces, LANES * (-(-width // (pieces * LANES)))
    return -(-most // ROWS) * ROWS, 0, 0


def fold(rows, blocks, kept, pieces, piece, width):
    main = rows[: blocks * kept]
    if not pieces:
        return main.reshape(blocks, kept, width)
    further = rows[blocks * kept :]
    main = jnp.pad(main, ((0, 0), (0, -width % LANES)))
    further = jnp.pad(further, ((0, 0), (0, pieces * piece - width))).reshape(blocks * kept, piece)
    return jnp.concatenate([main, further], axis=1).reshape(blocks, kept, -1)


def unfold(blocks_in, blocks, kept, pieces, piece, width):
    flat = blocks_in.reshape(blocks * kept, -1)
    if not pieces:
        return flat
    main = flat[:, :width]
    further = flat[:, width + -width % LANES :].reshape(-1, pieces * piece)[:, :width]
    return jnp.concatenate([main, further], axis=0)


def body(tokens, expert_ids, route_weights, w_gate, w_up, w_down):
    experts = EXP_SITE * lax.axis_size("site")
    split = lax.axis_size("member") // EXP_SITE
    count, width = tokens.shape
    mean_rows = count * expert_ids.shape[1] // experts
    most = mean_rows + max(1, mean_rows // 8)
    blocks = experts * split
    kept, pieces, piece = fold_plan(most, width)
    plan = (blocks, kept, pieces, piece, width)
    total = most if pieces else kept

    def ordered(table):
        table = jnp.repeat(table, split, axis=0)
        parts = [table[:, :kept], table[:, kept:]] if pieces else [table]
        return jnp.concatenate([p.reshape(-1, count) for p in parts], axis=0)

    select, weights = routing(expert_ids, route_weights, experts, total)
    packed = jnp.dot(ordered(select), tokens, preferred_element_type=jnp.float32).astype(jnp.bfloat16)
    received = lax.all_to_all(fold(packed, *plan), AXES, split_axis=0, concat_axis=0, tiled=True)
    produced = expert_apply(unfold(received, *plan), w_gate[0], w_up[0], w_down[0])
    returned = lax.all_to_all(fold(produced, *plan), AXES, split_axis=0, concat_axis=0, tiled=True)
    mixed = lax.dot_general(
        ordered(weights), unfold(returned, *plan), (((0,), (0,)), ((), ())), preferred_element_type=jnp.float32
    )
    return mixed.astype(jnp.bfloat16)


def solution(mesh):
    rows = P(("groups", "site", "member"), None)
    held = P(("site", "member"), None, None)
    return jax.shard_map(
        body,
        mesh=mesh,
        in_specs=(rows, rows, rows, held, held, held),
        out_specs=rows,
        check_vma=False,
    )
```

```python
import functools

import jax
import jax.numpy as jnp
from jax import lax
from jax.experimental import pallas as pl
from jax.experimental.pallas import tpu as pltpu
from jax.sharding import PartitionSpec as P

EXP_SITE = 4
ALPHA = 1.702
AXES = ("site", "member")
ROWS, LANES = 16, 128
CHUNK = 512


def routing(expert_ids, route_weights, experts, most):
    count = expert_ids.shape[0]
    columns = lax.broadcasted_iota(jnp.int32, (1, 1, experts), 2)
    matches = expert_ids[:, :, None] == columns
    hit = jnp.any(matches, axis=1)
    table = jnp.sum(jnp.where(matches, route_weights[:, :, None].astype(jnp.float32), 0.0), axis=1)
    row = lax.broadcasted_iota(jnp.int32, (count, count), 0)
    col = lax.broadcasted_iota(jnp.int32, (count, count), 1)
    before = (col < row).astype(jnp.bfloat16)
    position = lax.dot_general(
        hit.astype(jnp.bfloat16), before, (((0,), (1,)), ((), ())), preferred_element_type=jnp.float32
    ).astype(jnp.int32)
    slot = lax.broadcasted_iota(jnp.int32, (experts, most, count), 1)
    chosen = (position[:, None, :] == slot) & hit.T[:, None, :]
    select = chosen.astype(jnp.bfloat16)
    weights = jnp.where(chosen, table.T[:, None, :], 0.0).astype(jnp.bfloat16)
    return select, weights


def expert_kernel(tail, x_ref, gate_ref, up_ref, down_ref, out_ref, total_ref):
    step = pl.program_id(1)
    steps = pl.num_programs(1)

    def term(valid):
        rows = x_ref[...]
        gate = jnp.dot(rows, gate_ref[0, :, :valid], preferred_element_type=jnp.float32)
        up = jnp.dot(rows, up_ref[0, :, :valid], preferred_element_type=jnp.float32)
        hidden = ((up + 1.0) * gate * jax.nn.sigmoid(ALPHA * gate)).astype(jnp.bfloat16)
        return jnp.dot(hidden, down_ref[0, :valid, :], preferred_element_type=jnp.float32)

    @pl.when(step == 0)
    def _():
        total_ref[...] = jnp.zeros_like(total_ref)

    @pl.when(step < steps - 1)
    def _():
        total_ref[...] += term(CHUNK)

    @pl.when(step == steps - 1)
    def _():
        out_ref[...] = (total_ref[...] + term(tail)).astype(out_ref.dtype)


def expert_apply(rows, w_gate, w_up, w_down):
    count, width = rows.shape
    hidden = w_gate.shape[2]
    steps = -(-hidden // CHUNK)
    block = max(b for b in range(ROWS, min(count, 512) + 1, ROWS) if count % b == 0)
    return pl.pallas_call(
        functools.partial(expert_kernel, hidden - (steps - 1) * CHUNK),
        grid=(count // block, steps),
        in_specs=[
            pl.BlockSpec((block, width), lambda r, f: (r, 0)),
            pl.BlockSpec((1, width, CHUNK), lambda r, f: (0, 0, f)),
            pl.BlockSpec((1, width, CHUNK), lambda r, f: (0, 0, f)),
            pl.BlockSpec((1, CHUNK, width), lambda r, f: (0, f, 0)),
        ],
        out_specs=pl.BlockSpec((block, width), lambda r, f: (r, 0)),
        out_shape=jax.ShapeDtypeStruct((count, width), jnp.bfloat16),
        scratch_shapes=[pltpu.VMEM((block, width), jnp.float32)],
        compiler_params=pltpu.CompilerParams(vmem_limit_bytes=48 * 1024 * 1024),
        cost_estimate=pl.CostEstimate(
            flops=6 * count * width * hidden,
            bytes_accessed=6 * width * hidden + 4 * count * width,
            transcendentals=count * hidden,
        ),
    )(rows, w_gate, w_up, w_down)


def fold_plan(most, width):
    extra = most % ROWS
    if most > ROWS and extra and ROWS % extra == 0 and most // ROWS == 1:
        pieces = ROWS // extra
        return ROWS, pieces, LANES * (-(-width // (pieces * LANES)))
    return -(-most // ROWS) * ROWS, 0, 0


def fold(rows, blocks, kept, pieces, piece, width):
    main = rows[: blocks * kept]
    if not pieces:
        return main.reshape(blocks, kept, width)
    further = rows[blocks * kept :]
    main = jnp.pad(main, ((0, 0), (0, -width % LANES)))
    further = jnp.pad(further, ((0, 0), (0, pieces * piece - width))).reshape(blocks * kept, piece)
    return jnp.concatenate([main, further], axis=1).reshape(blocks, kept, -1)


def unfold(blocks_in, blocks, kept, pieces, piece, width):
    flat = blocks_in.reshape(blocks * kept, -1)
    if not pieces:
        return flat
    main = flat[:, :width]
    further = flat[:, width + -width % LANES :].reshape(-1, pieces * piece)[:, :width]
    return jnp.concatenate([main, further], axis=0)


def body(tokens, expert_ids, route_weights, w_gate, w_up, w_down):
    experts = EXP_SITE * lax.axis_size("site")
    split = lax.axis_size("member") // EXP_SITE
    count, width = tokens.shape
    mean_rows = count * expert_ids.shape[1] // experts
    most = mean_rows + max(1, mean_rows // 8)
    blocks = experts * split
    kept, pieces, piece = fold_plan(most, width)
    plan = (blocks, kept, pieces, piece, width)
    total = most if pieces else kept

    def ordered(table):
        table = jnp.repeat(table, split, axis=0)
        parts = [table[:, :kept], table[:, kept:]] if pieces else [table]
        return jnp.concatenate([p.reshape(-1, count) for p in parts], axis=0)

    select, weights = routing(expert_ids, route_weights, experts, total)
    packed = jnp.dot(ordered(select), tokens, preferred_element_type=jnp.float32).astype(jnp.bfloat16)
    received = lax.all_to_all(fold(packed, *plan), AXES, split_axis=0, concat_axis=0, tiled=True)
    produced = expert_apply(unfold(received, *plan), w_gate, w_up, w_down)
    returned = lax.all_to_all(fold(produced, *plan), AXES, split_axis=0, concat_axis=0, tiled=True)
    mixed = lax.dot_general(
        ordered(weights), unfold(returned, *plan), (((0,), (0,)), ((), ())), preferred_element_type=jnp.float32
    )
    return mixed.astype(jnp.bfloat16)


def solution(mesh):
    rows = P(("groups", "site", "member"), None)
    held = P(("site", "member"), None, None)
    return jax.shard_map(
        body,
        mesh=mesh,
        in_specs=(rows, rows, rows, held, held, held),
        out_specs=rows,
        check_vma=False,
    )
```

```python
import functools

import jax
import jax.numpy as jnp
from jax import lax
from jax.experimental import pallas as pl
from jax.experimental.pallas import tpu as pltpu
from jax.sharding import PartitionSpec as P

EXP_SITE = 4
ALPHA = 1.702
AXES = ("site", "member")
ROWS, LANES = 16, 128
CHUNK = 512


def routing(expert_ids, route_weights, experts, most):
    count = expert_ids.shape[0]
    columns = lax.broadcasted_iota(jnp.int32, (1, 1, experts), 2)
    matches = expert_ids[:, :, None] == columns
    hit = jnp.any(matches, axis=1)
    table = jnp.sum(jnp.where(matches, route_weights[:, :, None].astype(jnp.float32), 0.0), axis=1)
    row = lax.broadcasted_iota(jnp.int32, (count, count), 0)
    col = lax.broadcasted_iota(jnp.int32, (count, count), 1)
    before = (col < row).astype(jnp.bfloat16)
    position = lax.dot_general(
        hit.astype(jnp.bfloat16), before, (((0,), (1,)), ((), ())), preferred_element_type=jnp.float32
    ).astype(jnp.int32)
    slot = lax.broadcasted_iota(jnp.int32, (experts, most, count), 1)
    chosen = (position[:, None, :] == slot) & hit.T[:, None, :]
    select = chosen.astype(jnp.bfloat16)
    weights = jnp.where(chosen, table.T[:, None, :], 0.0).astype(jnp.bfloat16)
    return select, weights


def expert_kernel(tail, x_ref, gate_ref, up_ref, down_ref, out_ref, total_ref):
    step = pl.program_id(1)
    steps = pl.num_programs(1)

    def term(valid):
        rows = x_ref[...]
        gate = jnp.dot(rows, gate_ref[0, :, :valid], preferred_element_type=jnp.float32)
        up = jnp.dot(rows, up_ref[0, :, :valid], preferred_element_type=jnp.float32)
        hidden = ((up + 1.0) * gate * jax.nn.sigmoid(ALPHA * gate)).astype(jnp.bfloat16)
        return jnp.dot(hidden, down_ref[0, :valid, :], preferred_element_type=jnp.float32)

    @pl.when(step == 0)
    def _():
        total_ref[...] = jnp.zeros_like(total_ref)

    @pl.when(step < steps - 1)
    def _():
        total_ref[...] += term(CHUNK)

    @pl.when(step == steps - 1)
    def _():
        out_ref[...] = (total_ref[...] + term(tail)).astype(out_ref.dtype)


def expert_apply(rows, w_gate, w_up, w_down):
    count, width = rows.shape
    hidden = w_gate.shape[2]
    steps = -(-hidden // CHUNK)
    block = max(b for b in range(ROWS, min(count, 512) + 1, ROWS) if count % b == 0)
    return pl.pallas_call(
        functools.partial(expert_kernel, hidden - (steps - 1) * CHUNK),
        grid=(count // block, steps),
        in_specs=[
            pl.BlockSpec((block, width), lambda r, f: (r, 0)),
            pl.BlockSpec((1, width, CHUNK), lambda r, f: (0, 0, f)),
            pl.BlockSpec((1, width, CHUNK), lambda r, f: (0, 0, f)),
            pl.BlockSpec((1, CHUNK, width), lambda r, f: (0, f, 0)),
        ],
        out_specs=pl.BlockSpec((block, width), lambda r, f: (r, 0)),
        out_shape=jax.ShapeDtypeStruct((count, width), jnp.bfloat16),
        scratch_shapes=[pltpu.VMEM((block, width), jnp.float32)],
        compiler_params=pltpu.CompilerParams(vmem_limit_bytes=48 * 1024 * 1024),
        cost_estimate=pl.CostEstimate(
            flops=6 * count * width * hidden,
            bytes_accessed=6 * width * hidden + 4 * count * width,
            transcendentals=count * hidden,
        ),
    )(rows, w_gate, w_up, w_down)


def fold_plan(most, width):
    extra = most % ROWS
    if most > ROWS and extra and ROWS % extra == 0 and most // ROWS == 1:
        pieces = ROWS // extra
        return ROWS, pieces, LANES * (-(-width // (pieces * LANES)))
    return -(-most // ROWS) * ROWS, 0, 0


def fold(rows, blocks, kept, pieces, piece, width):
    main = rows[: blocks * kept]
    if not pieces:
        return main.reshape(blocks, kept, width)
    further = rows[blocks * kept :]
    main = jnp.pad(main, ((0, 0), (0, -width % LANES)))
    further = jnp.pad(further, ((0, 0), (0, pieces * piece - width))).reshape(blocks * kept, piece)
    return jnp.concatenate([main, further], axis=1).reshape(blocks, kept, -1)


def unfold(blocks_in, blocks, kept, pieces, piece, width):
    flat = blocks_in.reshape(blocks * kept, -1)
    if not pieces:
        return flat
    main = flat[:, :width]
    further = flat[:, width + -width % LANES :].reshape(-1, pieces * piece)[:, :width]
    return jnp.concatenate([main, further], axis=0)


def exchange_kernel(sites, members, src_ref, dst_ref, local_sem, send_sems, recv_sems):
    site, member = lax.axis_index("site"), lax.axis_index("member")
    me = site * members + member
    count = sites * members

    def place(k):
        to_site = lax.rem(site + k // members, sites)
        to_member = lax.rem(member + lax.rem(k, members), members)
        return to_site, to_member

    def origin(k):
        from_site = lax.rem(site + sites - k // members, sites)
        from_member = lax.rem(member + members - lax.rem(k, members), members)
        return from_site * members + from_member

    def copy(k, landing):
        to_site, to_member = place(k)
        return pltpu.make_async_remote_copy(
            src_ref=src_ref.at[to_site * members + to_member],
            dst_ref=dst_ref.at[landing],
            send_sem=send_sems.at[k],
            recv_sem=recv_sems.at[k],
            device_id={"site": to_site, "member": to_member},
            device_id_type=pl.DeviceIdType.MESH,
        )

    barrier = pltpu.get_barrier_semaphore()

    @pl.loop(1, count)
    def _(k):
        to_site, to_member = place(k)
        pl.semaphore_signal(
            barrier, inc=1, device_id={"site": to_site, "member": to_member}, device_id_type=pl.DeviceIdType.MESH
        )

    pl.semaphore_wait(barrier, count - 1)

    @pl.loop(1, count)
    def _(k):
        copy(count - k, me).start()

    own = pltpu.make_async_copy(src_ref.at[me], dst_ref.at[me], local_sem)
    own.start()
    own.wait()

    @pl.loop(1, count)
    def _(k):
        arriving = copy(k, origin(k))
        arriving.wait_send()
        arriving.wait_recv()


def exchange(blocks):
    sites, members = lax.axis_size("site"), lax.axis_size("member")
    count = sites * members
    return pl.pallas_call(
        functools.partial(exchange_kernel, sites, members),
        in_specs=[pl.BlockSpec(memory_space=pltpu.VMEM)],
        out_specs=pl.BlockSpec(memory_space=pltpu.VMEM),
        out_shape=jax.ShapeDtypeStruct(blocks.shape, blocks.dtype),
        scratch_shapes=[
            pltpu.SemaphoreType.DMA,
            pltpu.SemaphoreType.DMA((count,)),
            pltpu.SemaphoreType.DMA((count,)),
        ],
        compiler_params=pltpu.CompilerParams(
            collective_id=0, has_side_effects=True, vmem_limit_bytes=48 * 1024 * 1024
        ),
        cost_estimate=pl.CostEstimate(flops=0, bytes_accessed=4 * blocks.size, transcendentals=0),
    )(blocks)


def body(tokens, expert_ids, route_weights, w_gate, w_up, w_down):
    experts = EXP_SITE * lax.axis_size("site")
    split = lax.axis_size("member") // EXP_SITE
    count, width = tokens.shape
    mean_rows = count * expert_ids.shape[1] // experts
    most = mean_rows + max(1, mean_rows // 8)
    blocks = experts * split
    kept, pieces, piece = fold_plan(most, width)
    plan = (blocks, kept, pieces, piece, width)
    total = most if pieces else kept

    def ordered(table):
        table = jnp.repeat(table, split, axis=0)
        parts = [table[:, :kept], table[:, kept:]] if pieces else [table]
        return jnp.concatenate([p.reshape(-1, count) for p in parts], axis=0)

    select, weights = routing(expert_ids, route_weights, experts, total)
    packed = jnp.dot(ordered(select), tokens, preferred_element_type=jnp.float32).astype(jnp.bfloat16)
    received = exchange(fold(packed, *plan))
    produced = expert_apply(unfold(received, *plan), w_gate, w_up, w_down)
    returned = exchange(fold(produced, *plan))
    mixed = lax.dot_general(
        ordered(weights), unfold(returned, *plan), (((0,), (0,)), ((), ())), preferred_element_type=jnp.float32
    )
    return mixed.astype(jnp.bfloat16)


def solution(mesh):
    rows = P(("groups", "site", "member"), None)
    held = P(("site", "member"), None, None)
    return jax.shard_map(
        body,
        mesh=mesh,
        in_specs=(rows, rows, rows, held, held, held),
        out_specs=rows,
        check_vma=False,
    )
```
